256 devices in a mesh: dp: 4 (over z_hi), expert: 8 (over x, z_lo), tensor: 8 (over y, core).
Axes of the slice: x: 4, y: 4, z: 8 (z_hi: 4, z_lo: 2; z = z_hi * 2 + z_lo), core: 2. Of those that a mesh axis runs over, the one named last changes fastest.
Arguments:
- tokens: bfloat16 [3072, 3072], P(('dp', 'expert', 'tensor')), may hold values from -6 to 6
- grad_out: bfloat16 [3072, 3072], P(('dp', 'expert', 'tensor')), may hold values from -3 to 3
- gates: float32 [3072, 2], P(('dp', 'expert', 'tensor')), may hold values from 0.1 to 0.9
- expert_ids: int32 [3072, 2], P(('dp', 'expert')), may hold values from 0 to 7, all different within a row
- w_gate: bfloat16 [8, 3072, 8192], P('expert', None, ('dp', 'tensor')), may hold values from -0.109375 to 0.109375
- w_up: bfloat16 [8, 3072, 8192], P('expert', None, ('dp', 'tensor')), may hold values from -0.109375 to 0.109375
- w_down: bfloat16 [8, 3072, 8192], P('expert', None, ('dp', 'tensor')), may hold values from -0.0625 to 0.0625
Outputs:
- grad_tokens: bfloat16 [3072, 3072], P(('dp', 'expert', 'tensor'))
- grad_gate: bfloat16 [8, 3072, 8192], P('expert', None, ('dp', 'tensor'))
- grad_up: bfloat16 [8, 3072, 8192], P('expert', None, ('dp', 'tensor'))
- grad_down: bfloat16 [8, 3072, 8192], P('expert', None, ('dp', 'tensor'))
The draws below stay inside these ranges and needn't reach their ends.
Inputs may be any that keep to these rules, and one draw needn't show every extreme that they name: `expert_ids`: each token names 2 different experts, and every expert is named by some token.
All inputs are finite; a program needn't handle non-finite values.
Results may differ from the reference program's by a relative error of at most 0.017.
Values may be sent and summed in bfloat16 or wider, within the bound.
No kernel may reach another device: no remote copies, remote signals or barrier semaphores. Data moves between devices by JAX's collectives and lax.ppermute only.
A program may use at most 128 MiB of HBM per device.

```python
import jax
import jax.numpy as jnp
from jax import lax

D = 3072
FF = 8192
TOP = 2
TOK_GRP = 96
EXPERTS = 8
CAP = 32
TOKENS = 3072


def shard_levels(key, dims, split, low, largest):
    gain = 1.0
    for dim, parts in split:
        heights = jax.random.uniform(jax.random.fold_in(jax.random.fold_in(key, 6), dim), (parts,), jnp.float32, low / len(split), largest / len(split))
        gain = gain * jnp.repeat(jnp.exp(heights), dims[dim] // parts).reshape((-1,) + (1,) * (len(dims) - 1 - dim))
    return gain


def different_ones(rng, rows, amount, top, lift):
    sequence = jax.random.permutation(jax.random.fold_in(rng, 1), amount)
    pull = sequence
    for power in range(3):
        pull = pull * pull // amount
    pull = pull * lift // amount
    tickets = jax.random.randint(jax.random.fold_in(rng, 2), (rows, amount), 0, 4096) + pull
    holders = jax.random.permutation(jax.random.fold_in(rng, 3), rows)[jnp.arange(amount) % rows]
    tickets = jnp.where(jnp.arange(rows)[:, None] == holders[None, :], 1 << 14, tickets)
    score = tickets * amount + jnp.arange(amount)
    return lax.top_k(score.astype(jnp.int32), top)[1].astype(jnp.int32)


def centred(key, shape, width, limit, pieces=(), kind=jnp.bfloat16):
    array = width * jax.random.normal(key, shape, jnp.float32)
    if pieces:
        array = array * shard_levels(key, shape, pieces, -0.22, 0.18)
    return jnp.clip(array, -limit, limit).astype(kind)


def setup_inputs(seed: int = 0) -> dict:
    splits = jax.random.split(jax.random.key(seed), 8)
    return {
        "tokens": centred(splits[0], (TOKENS, D), 1.0, 6.0, ((0, 256),)),
        "grad_out": centred(splits[1], (TOKENS, D), 0.5, 3.0, ((0, 256),)),
        "gates": jnp.clip(0.1 + 0.79999997 * jax.random.uniform(splits[2], (TOKENS, TOP), jnp.float32) ** shard_levels(splits[2], (TOKENS, TOP), ((0, 256),), -0.2, 0.2), 0.1, 0.9),
        "expert_ids": different_ones(splits[3], TOKENS, EXPERTS, TOP, 4096),
        "w_gate": centred(splits[4], (EXPERTS, D, FF), D ** -0.5, 0.109375, ((0, 8), (2, 32))),
        "w_up": centred(splits[5], (EXPERTS, D, FF), D ** -0.5, 0.109375, ((0, 8), (2, 32))),
        "w_down": centred(splits[6], (EXPERTS, D, FF), FF ** -0.5, 0.0625, ((0, 8), (2, 32))),
    }


def dispatch_table(expert_ids):
    id_blocks = expert_ids.reshape(-1, TOK_GRP * TOP)
    onehot = (id_blocks[:, :, None] == jnp.arange(EXPERTS, dtype=jnp.int32)[None, None, :]).astype(jnp.int32)
    before = jnp.cumsum(onehot, axis=1) - onehot
    slot_index = jnp.sum(before * onehot, axis=2)
    target = jnp.where(slot_index < CAP, id_blocks * CAP + slot_index, EXPERTS * CAP)
    slot_table = target[:, :, None] == jnp.arange(EXPERTS * CAP, dtype=jnp.int32)[None, None, :]
    return slot_table.astype(jnp.float32)


def reference(tokens, grad_out, gates, expert_ids, w_gate, w_up, w_down):
    block_count = TOKENS // TOK_GRP
    slot_table = dispatch_table(expert_ids)
    rows_x = jnp.repeat(tokens.reshape(block_count, TOK_GRP, D), TOP, axis=1).astype(jnp.float32)
    scaled = gates.reshape(block_count, TOK_GRP * TOP, 1) * jnp.repeat(grad_out.reshape(block_count, TOK_GRP, D), TOP, axis=1).astype(jnp.float32)
    gated_rows = scaled.astype(jnp.bfloat16).astype(jnp.float32)
    x_buffer = jnp.einsum('bae,bad->bed', slot_table, rows_x).astype(jnp.bfloat16).reshape(block_count, EXPERTS, CAP, D)
    g_buffer = jnp.einsum('bae,bad->bed', slot_table, gated_rows).astype(jnp.bfloat16).reshape(block_count, EXPERTS, CAP, D)
    grads_gate, grads_up, grads_down, slot_list = [], [], [], []
    for expert in range(EXPERTS):
        slot_x = x_buffer[:, expert].reshape(block_count * CAP, D)
        slot_g = g_buffer[:, expert].reshape(block_count * CAP, D)
        h_gate = jnp.dot(slot_x, w_gate[expert], preferred_element_type=jnp.float32)
        h_up = jnp.dot(slot_x, w_up[expert], preferred_element_type=jnp.float32)
        d_act = jnp.dot(slot_g, w_down[expert], preferred_element_type=jnp.float32)
        sigmoid_gate = jax.nn.sigmoid(h_gate)
        activated = (h_gate * sigmoid_gate * h_up).astype(jnp.bfloat16)
        d_up = (d_act * h_gate * sigmoid_gate).astype(jnp.bfloat16)
        d_gate = (d_act * h_up * sigmoid_gate * (1.0 + h_gate * (1.0 - sigmoid_gate))).astype(jnp.bfloat16)
        grads_gate.append(jnp.dot(slot_x.T, d_gate, preferred_element_type=jnp.float32).astype(jnp.bfloat16))
        grads_up.append(jnp.dot(slot_x.T, d_up, preferred_element_type=jnp.float32).astype(jnp.bfloat16))
        grads_down.append(jnp.dot(slot_g.T, activated, preferred_element_type=jnp.float32).astype(jnp.bfloat16))
        backward = jnp.dot(d_gate, w_gate[expert].T, preferred_element_type=jnp.float32)
        backward = backward + jnp.dot(d_up, w_up[expert].T, preferred_element_type=jnp.float32)
        slot_list.append(backward.astype(jnp.bfloat16).reshape(block_count, CAP, D))
    slot_grads = jnp.stack(slot_list, axis=1).reshape(block_count, EXPERTS * CAP, D).astype(jnp.float32)
    per_assign = jnp.einsum('bae,bed->bad', slot_table, slot_grads)
    grad_tokens = jnp.sum(per_assign.reshape(block_count, TOK_GRP, TOP, D), axis=2).reshape(TOKENS, D).astype(jnp.bfloat16)
    return grad_tokens, jnp.stack(grads_gate), jnp.stack(grads_up), jnp.stack(grads_down)
```

```python
import jax
import jax.numpy as jnp
from jax import lax
from jax.sharding import PartitionSpec as P

TOP = 2
F32 = jnp.float32
BF16 = jnp.bfloat16


def dot(left, right, dims):
    return lax.dot_general(left, right, (dims, ((), ())), preferred_element_type=F32)


def send_y(array, step):
    chips = lax.axis_size("tensor") // 2
    pairs = [(2 * y + c, 2 * ((y + step) % chips) + c) for y in range(chips) for c in range(2)]
    return lax.ppermute(array, "tensor", pairs)


def send_dp(array, step):
    count = lax.axis_size("dp")
    return lax.ppermute(array, "dp", [(i, (i + step) % count) for i in range(count)])


def swap_cores(array):
    return lax.ppermute(array, "tensor", [(t, t ^ 1) for t in range(lax.axis_size("tensor"))])


def three_parts(gates):
    high = lax.reduce_precision(gates, 8, 7)
    rest = gates - high
    middle = lax.reduce_precision(rest, 8, 7)
    return jnp.concatenate([high, middle, rest - middle], axis=1).astype(BF16)


def routing(expert_ids, experts, member, capacity, slot_part):
    assigned = expert_ids.reshape(-1)
    onehot = (assigned[:, None] == jnp.arange(experts, dtype=jnp.int32)[None, :]).astype(jnp.int32)
    before = jnp.cumsum(onehot, axis=0) - onehot
    slot_index = jnp.sum(before * onehot, axis=1)
    target = jnp.where(slot_index < capacity, assigned * capacity + slot_index, -1)
    column = jnp.arange(experts * slot_part, dtype=jnp.int32)
    wanted = (column // slot_part) * capacity + member * slot_part + column % slot_part
    return (target[:, None] == wanted[None, :]).astype(BF16)


def gather_y(both, back, ahead, features):
    far_x = send_y(back[:, :features], 1)
    far_g = send_y(ahead[:, features:], -1)
    x = jnp.concatenate([both[:, :features], back[:, :features], far_x, ahead[:, :features]], 0)
    g = jnp.concatenate([both[:, features:], back[:, features:], far_g, ahead[:, features:]], 0)
    return x, g


def hidden_backward(x, g, gate_up, down):
    h = dot(x, gate_up, ((1,), (0,)))
    d_act = dot(g, down, ((1,), (0,)))
    width = down.shape[1]
    h_gate, h_up = h[:, :width], h[:, width:]
    s = jax.nn.sigmoid(h_gate)
    act = (h_gate * s * h_up).astype(BF16)
    d_up = (d_act * h_gate * s).astype(BF16)
    d_gate = (d_act * h_up * s * (1.0 + h_gate * (1.0 - s))).astype(BF16)
    back = dot(jnp.concatenate([d_gate, d_up], 1), gate_up, ((1,), (1,))).astype(BF16)
    return act, d_gate, d_up, back


def sum_y(back):
    rows = back.shape[0] // 4
    total = back[:rows].astype(F32)
    for step in (1, 3, 2):
        total = total + send_y(back[step * rows : (step + 1) * rows], -step).astype(F32)
    return total.astype(BF16)


def local(tokens, grad_out, gates, expert_ids, w_gate, w_up, w_down):
    experts = w_gate.shape[0] * lax.axis_size("expert")
    members = lax.axis_size("tensor")
    member = lax.axis_index("tensor")
    chip, core = member // 2, member % 2
    own_rows, features = tokens.shape
    padded = -(-own_rows // 16) * 16
    group_size = own_rows * members
    capacity = (
        (5 * group_size * TOP + 4 * experts * members - 1) // (4 * experts * members) * members
    )
    slot_part = capacity // members
    part_slots = experts * slot_part

    packed = jnp.concatenate([tokens, grad_out, three_parts(gates)], axis=1)
    packed = jnp.pad(packed, ((0, padded - own_rows), (0, 128 - 3 * TOP)))
    pieces = [packed] + [send_y(packed, step) for step in (1, 3, 2)]
    pieces = pieces + [swap_cores(piece) for piece in pieces]
    rows = jnp.concatenate(pieces, axis=0)

    gate, up, down = w_gate[0], w_up[0], w_down[0]
    gate2, up2, down2 = swap_cores(gate), swap_cores(up), swap_cores(down)

    table = routing(expert_ids, experts, member, capacity, slot_part)
    table = table.reshape(members, own_rows, TOP, part_slots)
    order = jnp.stack(
        [2 * ((chip - step) % (members // 2)) + c for c in (core, 1 - core) for step in (0, 1, 3, 2)]
    )
    here = jnp.pad(table[order], ((0, 0), (0, padded - own_rows), (0, 0), (0, 0)))
    here = here.reshape(members * padded, TOP, part_slots)
    pick = jnp.sum(here, axis=1)
    second = jnp.sum(here[:, 1].astype(F32), axis=0)[:, None] > 0
    found = dot(pick, rows, ((0,), (0,)))
    parts = found[:, 2 * features :]
    gate_pair = parts[:, 0:2] + parts[:, 2:4] + parts[:, 4:6]
    slot_gate = jnp.where(second, gate_pair[:, 1:2], gate_pair[:, 0:1])
    slots = jnp.concatenate(
        [found[:, :features], slot_gate * found[:, features : 2 * features]], axis=1
    ).astype(BF16)

    slots, gate2, up2, down2 = lax.optimization_barrier((slots, gate2, up2, down2))
    gate_up = jnp.concatenate([gate, gate2, up, up2], axis=1)
    down_all = jnp.concatenate([down, down2], axis=1)
    slots = slots.reshape(experts, slot_part, 2 * features)
    both0 = lax.all_to_all(slots, "expert", 0, 0, tiled=True).reshape(part_slots, 2 * features)
    both1, both3 = send_dp(both0, 1), send_dp(both0, -1)
    back0, ahead0 = send_y(both0, 1), send_y(both0, -1)
    both1, both3, back0, ahead0 = lax.optimization_barrier((both1, both3, back0, ahead0))
    x_far, g_far = send_dp(both1[:, :features], 1), send_dp(both3[:, features:], -1)
    near = jnp.concatenate([both1, both3], axis=0)
    back1, ahead1 = send_y(near, 1), send_y(near, -1)
    both2 = jnp.concatenate([x_far, g_far], axis=1)
    both2, back1, ahead1 = lax.optimization_barrier((both2, back1, ahead1))
    back2, ahead2 = send_y(both2, 1), send_y(both2, -1)
    results, xs, gs = [], [], []
    for trio in ((both0, back0, ahead0), (near, back1, ahead1), (both2, back2, ahead2)):
        x, g = gather_y(*trio, features)
        xs.append(x)
        gs.append(g)
        results.append(hidden_backward(x, g, gate_up, down_all))
    sums = [sum_y(r[3]) for r in results]

    near, far = sums[1][:part_slots], sums[1][part_slots:]
    by_step = [sums[0], near, sums[2], far]
    ring = jnp.concatenate([by_step[i % 4] for i in (3, 2, 1, 0, 3, 2, 1)], axis=0)
    by_dp = lax.dynamic_slice_in_dim(ring, (3 - lax.axis_index("dp")) * part_slots, 4 * part_slots)
    by_dp = by_dp.reshape(4 * experts, slot_part, features)
    returned = lax.all_to_all(by_dp, ("dp", "expert"), 0, 0, tiled=True)
    returned = returned.reshape(4 * part_slots, features)
    put = jnp.sum(table, axis=2).reshape(group_size, part_slots)
    terms = dot(jnp.tile(put, (1, 4)), returned, ((1,), (0,))).astype(BF16)
    terms = lax.all_to_all(
        terms.reshape(members, own_rows, features), "tensor", 0, 0, tiled=True
    )
    grad_tokens = jnp.sum(terms.astype(F32), axis=0).astype(BF16)

    x, g = jnp.concatenate(xs, axis=0), jnp.concatenate(gs, axis=0)
    act, d_gate, d_up = (jnp.concatenate([r[i] for r in results], axis=0) for i in range(3))
    width = gate.shape[1]

    def gradient(rows, cols):
        other = swap_cores(dot(rows, cols[:, width:], ((0,), (0,))).astype(BF16))
        own = dot(rows, cols[:, :width], ((0,), (0,)))
        return (own + other.astype(F32)).astype(BF16)[None]

    return (grad_tokens, gradient(x, d_gate), gradient(x, d_up), gradient(g, act))


def solution(mesh):
    in_specs = (
        P(("dp", "expert", "tensor"), None),
        P(("dp", "expert", "tensor"), None),
        P(("dp", "expert", "tensor"), None),
        P(("dp", "expert"), None),
        P("expert", None, ("dp", "tensor")),
        P("expert", None, ("dp", "tensor")),
        P("expert", None, ("dp", "tensor")),
    )
    out_specs = (
        P(("dp", "expert", "tensor"), None),
        P("expert", None, ("dp", "tensor")),
        P("expert", None, ("dp", "tensor")),
        P("expert", None, ("dp", "tensor")),
    )
    return jax.shard_map(local, mesh=mesh, in_specs=in_specs, out_specs=out_specs, check_vma=False)
```

```python
import jax
import jax.numpy as jnp
from jax import lax
from jax.sharding import PartitionSpec as P

TOP = 2
F32 = jnp.float32
BF16 = jnp.bfloat16


def dot(left, right, dims):
    return lax.dot_general(left, right, (dims, ((), ())), preferred_element_type=F32)


def send_y(array, step):
    chips = lax.axis_size("tensor") // 2
    pairs = [(2 * y + c, 2 * ((y + step) % chips) + c) for y in range(chips) for c in range(2)]
    return lax.ppermute(array, "tensor", pairs)


def send_dp(array, step):
    count = lax.axis_size("dp")
    return lax.ppermute(array, "dp", [(i, (i + step) % count) for i in range(count)])


def swap_cores(array):
    return lax.ppermute(array, "tensor", [(t, t ^ 1) for t in range(lax.axis_size("tensor"))])


def three_parts(gates):
    high = lax.reduce_precision(gates, 8, 7)
    rest = gates - high
    middle = lax.reduce_precision(rest, 8, 7)
    return jnp.concatenate([high, middle, rest - middle], axis=1).astype(BF16)


def routing(expert_ids, experts, member, capacity, slot_part):
    assigned = expert_ids.reshape(-1)
    onehot = (assigned[:, None] == jnp.arange(experts, dtype=jnp.int32)[None, :]).astype(jnp.int32)
    before = jnp.cumsum(onehot, axis=0) - onehot
    slot_index = jnp.sum(before * onehot, axis=1)
    target = jnp.where(slot_index < capacity, assigned * capacity + slot_index, -1)
    column = jnp.arange(experts * slot_part, dtype=jnp.int32)
    wanted = (column // slot_part) * capacity + member * slot_part + column % slot_part
    return (target[:, None] == wanted[None, :]).astype(BF16)


def far_y(back, ahead):
    half = back.shape[1] // 2
    return send_y(back[:, :half], 1), send_y(ahead[:, half:], -1)


def halves(here, back, far_x, far_g, ahead):
    half = here.shape[1] // 2
    x = jnp.concatenate([here[:, :half], back[:, :half], far_x, ahead[:, :half]], axis=0)
    g = jnp.concatenate([here[:, half:], back[:, half:], far_g, ahead[:, half:]], axis=0)
    return x, g


def hidden_backward(x, g, gate_up, down):
    h = dot(x, gate_up, ((1,), (0,)))
    d_act = dot(g, down, ((1,), (0,)))
    width = down.shape[1]
    h_gate, h_up = h[:, :width], h[:, width:]
    s = jax.nn.sigmoid(h_gate)
    act = (h_gate * s * h_up).astype(BF16)
    d_up = (d_act * h_gate * s).astype(BF16)
    d_gate = (d_act * h_up * s * (1.0 + h_gate * (1.0 - s))).astype(BF16)
    back = dot(jnp.concatenate([d_gate, d_up], 1), gate_up, ((1,), (1,))).astype(BF16)
    return act, d_gate, d_up, back


def total(*arrays):
    return sum(a.astype(F32) for a in arrays).astype(BF16)


def local(tokens, grad_out, gates, expert_ids, w_gate, w_up, w_down):
    experts = w_gate.shape[0] * lax.axis_size("expert")
    members = lax.axis_size("tensor")
    member = lax.axis_index("tensor")
    chip, core = member // 2, member % 2
    own_rows, features = tokens.shape
    group_size = own_rows * members
    capacity = (
        (5 * group_size * TOP + 4 * experts * members - 1) // (4 * experts * members) * members
    )
    slot_part = capacity // members
    part_slots = experts * slot_part

    gates_in = jnp.pad(three_parts(gates), ((0, own_rows), (0, 128 - 3 * TOP)))
    packed = jnp.concatenate([jnp.concatenate([tokens, grad_out], axis=0), gates_in], axis=1)
    pieces = [packed] + [send_y(packed, step) for step in (1, 3, 2)]
    pieces = pieces + [swap_cores(piece) for piece in pieces]
    rows = jnp.concatenate(pieces, axis=0)

    gate, up, down = w_gate[0], w_up[0], w_down[0]
    gate2, up2, down2 = swap_cores(gate), swap_cores(up), swap_cores(down)

    table = routing(expert_ids, experts, member, capacity, slot_part)
    table = table.reshape(members, own_rows, TOP, part_slots)
    order = jnp.stack(
        [2 * ((chip - step) % (members // 2)) + c for c in (core, 1 - core) for step in (0, 1, 3, 2)]
    )
    here = table[order]
    pick = jnp.sum(here, axis=2)
    x_pick = jnp.pad(pick, ((0, 0), (0, own_rows), (0, 0))).reshape(-1, part_slots)
    g_pick = jnp.pad(pick, ((0, 0), (own_rows, 0), (0, 0))).reshape(-1, part_slots)
    second = jnp.sum(here[:, :, 1].astype(F32), axis=(0, 1))[:, None] > 0
    found_x = dot(x_pick, rows, ((0,), (0,)))
    found_g = dot(g_pick, rows[:, :features], ((0,), (0,)))
    parts = found_x[:, features:]
    gate_pair = parts[:, 0:2] + parts[:, 2:4] + parts[:, 4:6]
    slot_gate = jnp.where(second, gate_pair[:, 1:2], gate_pair[:, 0:1])
    slots = jnp.concatenate([found_x[:, :features], slot_gate * found_g], axis=1).astype(BF16)

    slots, gate2, up2, down2 = lax.optimization_barrier((slots, gate2, up2, down2))
    gate_up = jnp.concatenate([gate, gate2, up, up2], axis=1)
    down_all = jnp.concatenate([down, down2], axis=1)
    slots = slots.reshape(experts, slot_part, 2 * features)
    both0 = lax.all_to_all(slots, "expert", 0, 0, tiled=True).reshape(part_slots, 2 * features)
    both1, both3 = send_dp(both0, 1), send_dp(both0, -1)
    back0, ahead0, far0 = send_y(both0, 1), send_y(both0, -1), send_y(both0, 2)
    both1, both3, back0, ahead0, far0 = lax.optimization_barrier(
        (both1, both3, back0, ahead0, far0)
    )
    x_far, g_far = send_dp(both1[:, :features], 1), send_dp(both3[:, features:], -1)
    near = jnp.concatenate([both1, both3], axis=0)
    back1, ahead1 = send_y(near, 1), send_y(near, -1)
    both2 = jnp.concatenate([x_far, g_far], axis=1)
    both2, back0, far0 = lax.optimization_barrier((both2, back0, far0))
    far1 = jnp.concatenate([send_dp(far0, 1), send_dp(far0, -1)], axis=0)
    back2, ahead2 = send_y(both2, 1), send_y(both2, -1)

    x0, g0 = halves(both0, back0, far0[:, :features], far0[:, features:], ahead0)
    part0 = hidden_backward(x0, g0, gate_up, down_all)
    terms0, far1 = lax.optimization_barrier((part0[3], far1))
    here0, back_t0, far_t0, ahead_t0 = jnp.split(terms0, 4, axis=0)
    sum0 = total(here0, send_y(back_t0, -1), send_y(ahead_t0, 1))

    x1, g1 = halves(near, back1, far1[:, :features], far1[:, features:], ahead1)
    part1 = hidden_backward(x1, g1, gate_up, down_all)
    terms1, sum0, back2, ahead2 = lax.optimization_barrier((part1[3], sum0, back2, ahead2))
    far2_x, far2_g = far_y(back2, ahead2)
    far_t1 = terms1[4 * part_slots : 6 * part_slots]
    far2_x, far2_g, far_t1 = lax.optimization_barrier((far2_x, far2_g, far_t1))
    x2, g2 = halves(both2, back2, far2_x, far2_g, ahead2)
    part2 = hidden_backward(x2, g2, gate_up, down_all)

    n = part_slots
    here1, back_t1, _, ahead_t1 = jnp.split(terms1, 4, axis=0)
    far_t0 = total(far_t0, send_dp(far_t1[:n], -1), send_dp(far_t1[n:], 1))
    sum1 = total(here1, send_y(back_t1, -1), send_y(ahead_t1, 1))
    sum1, far_t0, terms2 = lax.optimization_barrier((sum1, far_t0, part2[3]))
    here2, back_t2, far_t2, ahead_t2 = jnp.split(terms2, 4, axis=0)
    far_t = send_y(jnp.concatenate([far_t2, far_t0], axis=0), 2)
    sum2 = total(here2, send_y(back_t2, -1), send_y(ahead_t2, 1), far_t[:n])
    from_a, from_b = send_dp(sum1[:n], -1), send_dp(sum1[n:], 1)
    from_2 = send_dp(sum2, 2)
    sums = total(sum0, far_t[n:], from_a, from_b, from_2)

    x = jnp.concatenate([x0, x1, x2], axis=0)
    g = jnp.concatenate([g0, g1, g2], axis=0)
    act, d_gate, d_up = (
        jnp.concatenate([part0[i], part1[i], part2[i]], axis=0) for i in range(3)
    )
    width = gate.shape[1]
    sides = ((x, d_gate), (x, d_up), (g, act))
    sides, sum2 = lax.optimization_barrier((sides, sum2))
    theirs = [dot(a, b[:, width:], ((0,), (0,))).astype(BF16) for a, b in sides]
    sums, theirs = lax.optimization_barrier((sums, theirs))
    other = [swap_cores(t) for t in theirs]

    returned = lax.all_to_all(
        sums.reshape(experts, slot_part, features), "expert", 0, 0, tiled=True
    ).reshape(part_slots, features)
    returned, other = lax.optimization_barrier((returned, other))
    put = jnp.pad(jnp.sum(table, axis=2), ((0, 0), (0, -own_rows % 8), (0, 0)))
    terms = dot(put.reshape(-1, part_slots), returned, ((1,), (0,))).astype(BF16)
    terms, sides = lax.optimization_barrier((terms, sides))
    own = [dot(a, b[:, :width], ((0,), (0,))) for a, b in sides]
    terms = lax.all_to_all(
        terms.reshape(members, -1, features), "tensor", 0, 0, tiled=True
    )
    grad_tokens = jnp.sum(terms.astype(F32), axis=0)[:own_rows].astype(BF16)

    grads = [(a + b.astype(F32)).astype(BF16)[None] for a, b in zip(own, other)]
    return (grad_tokens, *grads)


def solution(mesh):
    in_specs = (
        P(("dp", "expert", "tensor"), None),
        P(("dp", "expert", "tensor"), None),
        P(("dp", "expert", "tensor"), None),
        P(("dp", "expert"), None),
        P("expert", None, ("dp", "tensor")),
        P("expert", None, ("dp", "tensor")),
        P("expert", None, ("dp", "tensor")),
    )
    out_specs = (
        P(("dp", "expert", "tensor"), None),
        P("expert", None, ("dp", "tensor")),
        P("expert", None, ("dp", "tensor")),
        P("expert", None, ("dp", "tensor")),
    )
    return jax.shard_map(local, mesh=mesh, in_specs=in_specs, out_specs=out_specs, check_vma=False)
```

```python
import jax
import jax.numpy as jnp
from jax import lax
from jax.sharding import PartitionSpec as P

TOP = 2
F32 = jnp.float32
BF16 = jnp.bfloat16


def dot(left, right, dims):
    return lax.dot_general(left, right, (dims, ((), ())), preferred_element_type=F32)


def send_y(array, step):
    chips = lax.axis_size("tensor") // 2
    pairs = [(2 * y + c, 2 * ((y + step) % chips) + c) for y in range(chips) for c in range(2)]
    return lax.ppermute(array, "tensor", pairs)


def send_dp(array, step):
    count = lax.axis_size("dp")
    return lax.ppermute(array, "dp", [(i, (i + step) % count) for i in range(count)])


def swap_cores(array):
    return lax.ppermute(array, "tensor", [(t, t ^ 1) for t in range(lax.axis_size("tensor"))])


def three_parts(gates):
    high = lax.reduce_precision(gates, 8, 7)
    rest = gates - high
    middle = lax.reduce_precision(rest, 8, 7)
    return jnp.concatenate([high, middle, rest - middle], axis=1).astype(BF16)


def routing(expert_ids, experts, member, capacity, slot_part):
    assigned = expert_ids.reshape(-1)
    onehot = (assigned[:, None] == jnp.arange(experts, dtype=jnp.int32)[None, :]).astype(jnp.int32)
    before = jnp.cumsum(onehot, axis=0) - onehot
    slot_index = jnp.sum(before * onehot, axis=1)
    target = jnp.where(slot_index < capacity, assigned * capacity + slot_index, -1)
    column = jnp.arange(experts * slot_part, dtype=jnp.int32)
    wanted = (column // slot_part) * capacity + member * slot_part + column % slot_part
    return (target[:, None] == wanted[None, :]).astype(BF16)


def far_y(back, ahead):
    half = back.shape[1] // 2
    return send_y(back[:, :half], 1), send_y(ahead[:, half:], -1)


def halves(here, back, far_x, far_g, ahead):
    half = here.shape[1] // 2
    x = jnp.concatenate([here[:, :half], back[:, :half], far_x, ahead[:, :half]], axis=0)
    g = jnp.concatenate([here[:, half:], back[:, half:], far_g, ahead[:, half:]], axis=0)
    return x, g


def hidden_backward(x, g, gate_up, down):
    h = dot(x, gate_up, ((1,), (0,)))
    d_act = dot(g, down, ((1,), (0,)))
    width = down.shape[1]
    h_gate, h_up = h[:, :width], h[:, width:]
    s = jax.nn.sigmoid(h_gate)
    act = (h_gate * s * h_up).astype(BF16)
    d_up = (d_act * h_gate * s).astype(BF16)
    d_gate = (d_act * h_up * s * (1.0 + h_gate * (1.0 - s))).astype(BF16)
    back = dot(jnp.concatenate([d_gate, d_up], 1), gate_up, ((1,), (1,))).astype(BF16)
    return act, d_gate, d_up, back


def total(*arrays):
    return sum(a.astype(F32) for a in arrays).astype(BF16)


def local(tokens, grad_out, gates, expert_ids, w_gate, w_up, w_down):
    experts = w_gate.shape[0] * lax.axis_size("expert")
    members = lax.axis_size("tensor")
    member = lax.axis_index("tensor")
    chip, core = member // 2, member % 2
    own_rows, features = tokens.shape
    group_size = own_rows * members
    capacity = (
        (5 * group_size * TOP + 4 * experts * members - 1) // (4 * experts * members) * members
    )
    slot_part = capacity // members
    part_slots = experts * slot_part

    gates_in = jnp.pad(three_parts(gates), ((0, own_rows), (0, 128 - 3 * TOP)))
    packed = jnp.concatenate([jnp.concatenate([tokens, grad_out], axis=0), gates_in], axis=1)
    pieces = [packed] + [send_y(packed, step) for step in (1, 3, 2)]
    pieces = pieces + [swap_cores(piece) for piece in pieces]
    rows = jnp.concatenate(pieces, axis=0)

    gate, up, down = w_gate[0], w_up[0], w_down[0]
    gate2, up2, down2 = swap_cores(gate), swap_cores(up), swap_cores(down)

    table = routing(expert_ids, experts, member, capacity, slot_part)
    table = table.reshape(members, own_rows, TOP, part_slots)
    order = jnp.stack(
        [2 * ((chip - step) % (members // 2)) + c for c in (core, 1 - core) for step in (0, 1, 3, 2)]
    )
    here = table[order]
    pick = jnp.sum(here, axis=2)
    x_pick = jnp.pad(pick, ((0, 0), (0, own_rows), (0, 0))).reshape(-1, part_slots)
    g_pick = jnp.pad(pick, ((0, 0), (own_rows, 0), (0, 0))).reshape(-1, part_slots)
    second = jnp.sum(here[:, :, 1].astype(F32), axis=(0, 1))[:, None] > 0
    found_x = dot(x_pick, rows, ((0,), (0,)))
    found_g = dot(g_pick, rows[:, :features], ((0,), (0,)))
    parts = found_x[:, features:]
    gate_pair = parts[:, 0:2] + parts[:, 2:4] + parts[:, 4:6]
    slot_gate = jnp.where(second, gate_pair[:, 1:2], gate_pair[:, 0:1])
    slots = jnp.concatenate([found_x[:, :features], slot_gate * found_g], axis=1).astype(BF16)

    slots, gate2, up2, down2 = lax.optimization_barrier((slots, gate2, up2, down2))
    gate_up = jnp.concatenate([gate, gate2, up, up2], axis=1)
    down_all = jnp.concatenate([down, down2], axis=1)
    slots = slots.reshape(experts, slot_part, 2 * features)
    both0 = lax.all_to_all(slots, "expert", 0, 0, tiled=True).reshape(part_slots, 2 * features)
    both1, both3 = send_dp(both0, 1), send_dp(both0, -1)
    back0, ahead0, far0 = send_y(both0, 1), send_y(both0, -1), send_y(both0, 2)
    both1, both3, back0, ahead0, far0 = lax.optimization_barrier(
        (both1, both3, back0, ahead0, far0)
    )
    n = part_slots
    x_far, g_far = send_dp(both1[:, :features], 1), send_dp(both3[:, features:], -1)
    near = jnp.concatenate([both1, both3], axis=0)
    back1, ahead1 = send_y(near, 1), send_y(near, -1)
    both2 = jnp.concatenate([x_far, g_far], axis=1)
    both2, back0, far0, ahead0 = lax.optimization_barrier((both2, back0, far0, ahead0))
    back2, ahead2 = send_y(both2, 1), send_y(both2, -1)
    x0, g0 = halves(both0, back0, far0[:, :features], far0[:, features:], ahead0)
    part0 = hidden_backward(x0, g0, gate_up, down_all)
    terms0, back2, ahead2 = lax.optimization_barrier((part0[3], back2, ahead2))
    far2_x, far2_g = far_y(back2, ahead2)
    x2, g2 = halves(both2, back2, far2_x, far2_g, ahead2)
    part2 = hidden_backward(x2, g2, gate_up, down_all)
    far1_x, far1_g = far_y(back1, ahead1)
    terms2, far1_x, far1_g = lax.optimization_barrier((part2[3], far1_x, far1_g))
    x1, g1 = halves(near, back1, far1_x, far1_g, ahead1)
    part1 = hidden_backward(x1, g1, gate_up, down_all)

    here0, back_t0, far_t0, ahead_t0 = jnp.split(terms0, 4, axis=0)
    here2, back_t2, far_t2, ahead_t2 = jnp.split(terms2, 4, axis=0)
    here1, back_t1, far_t1, ahead_t1 = jnp.split(part1[3], 4, axis=0)
    came_back = send_y(jnp.concatenate([back_t0, back_t2], axis=0), -1)
    came_ahead = send_y(jnp.concatenate([ahead_t0, ahead_t2], axis=0), 1)
    sum0 = total(here0, came_back[:n], came_ahead[:n])
    sum2 = total(here2, came_back[n:], came_ahead[n:], send_y(far_t2, 2))
    sum1 = total(here1, send_y(back_t1, -1), send_y(ahead_t1, 1))
    sum2, sum0, far_t1 = lax.optimization_barrier((sum2, sum0, far_t1))
    far_t0 = total(far_t0, send_dp(far_t1[:n], -1), send_dp(far_t1[n:], 1))
    half = features // 2
    left, right = send_dp(sum2[:, :half], 1), send_dp(sum2[:, half:], -1)
    sum1, far_t0 = lax.optimization_barrier((sum1, far_t0))
    behind = jnp.concatenate([sum1[:n, :half], total(sum1[:n, half:], right)], axis=1)
    beyond = jnp.concatenate([total(sum1[n:, :half], left), sum1[n:, half:]], axis=1)
    from_a, from_b = send_dp(behind, -1), send_dp(beyond, 1)
    sums = total(sum0, send_y(far_t0, 2), from_a, from_b)

    x = jnp.concatenate([x0, x1, x2], axis=0)
    g = jnp.concatenate([g0, g1, g2], axis=0)
    act, d_gate, d_up = (
        jnp.concatenate([part0[i], part1[i], part2[i]], axis=0) for i in range(3)
    )
    width = gate.shape[1]
    sides = ((x, d_gate), (x, d_up), (g, act))
    sides, sum1 = lax.optimization_barrier((sides, sum1))
    theirs = [dot(a, b[:, width:], ((0,), (0,))).astype(BF16) for a, b in sides]
    sums, theirs = lax.optimization_barrier((sums, theirs))
    other = [swap_cores(t) for t in theirs]

    returned = lax.all_to_all(
        sums.reshape(experts, slot_part, features), "expert", 0, 0, tiled=True
    ).reshape(part_slots, features)
    returned, other = lax.optimization_barrier((returned, other))
    put = jnp.pad(jnp.sum(table, axis=2), ((0, 0), (0, -own_rows % 8), (0, 0)))
    terms = dot(put.reshape(-1, part_slots), returned, ((1,), (0,))).astype(BF16)
    terms, sides = lax.optimization_barrier((terms, sides))
    own = [dot(a, b[:, :width], ((0,), (0,))) for a, b in sides]
    terms = lax.all_to_all(
        terms.reshape(members, -1, features), "tensor", 0, 0, tiled=True
    )
    grad_tokens = jnp.sum(terms.astype(F32), axis=0)[:own_rows].astype(BF16)

    grads = [(a + b.astype(F32)).astype(BF16)[None] for a, b in zip(own, other)]
    return (grad_tokens, *grads)


def solution(mesh):
    in_specs = (
        P(("dp", "expert", "tensor"), None),
        P(("dp", "expert", "tensor"), None),
        P(("dp", "expert", "tensor"), None),
        P(("dp", "expert"), None),
        P("expert", None, ("dp", "tensor")),
        P("expert", None, ("dp", "tensor")),
        P("expert", None, ("dp", "tensor")),
    )
    out_specs = (
        P(("dp", "expert", "tensor"), None),
        P("expert", None, ("dp", "tensor")),
        P("expert", None, ("dp", "tensor")),
        P("expert", None, ("dp", "tensor")),
    )
    return jax.shard_map(local, mesh=mesh, in_specs=in_specs, out_specs=out_specs, check_vma=False)
```
